512 devices in a mesh: wide: 32 (over z, core), narrow: 16 (over x, y).
Axes of the slice: x: 4, y: 4, z: 16, core: 2. Of those that a mesh axis runs over, the one named last changes fastest.
Arguments:
- positions: float32 [16384, 3, 256], P(('wide', 'narrow')), may hold values from -1 to 1
- moments: float32 [16384, 3, 256], P(('wide', 'narrow')), may hold values from -6 to 6
- counts: int32 [16384], P(('wide', 'narrow')), may hold values from 1 to 256
- dest: int32 [16384], P(('wide', 'narrow')), may hold values from 0 to 15, as said below
Outputs:
- leaf_multipoles: float32 [65536, 286], P(('wide', 'narrow'))
- box_multipoles: float32 [13312, 286], P(('wide', 'narrow'))
The draws below stay inside these ranges and needn't reach their ends.
Inputs may be any that keep to these rules, and one draw needn't show every extreme that they name: `dest`: each device sends at most 8 of its blocks to one owner, and in every group one owner receives exactly 8 blocks from every device of the group.
All inputs are finite; a program needn't handle non-finite values.
Results may differ from the reference program's by a relative error of at most 0.0003.
Values sent between devices are 32-bit elements; how exact they have to be, the bound alone decides.
No kernel may reach another device: no remote copies, remote signals or barrier semaphores. Data moves between devices by JAX's collectives and lax.ppermute only.
A program may use at most 64 MiB of HBM per device.

```python
import math
import jax
import jax.numpy as jnp
import numpy as np
from jax import lax

P_SIZE = 10
PART = 256
LEVELS = 5
LEAF_DEV = 32
SLOT = 8
OWN_CAP = 128
BLOCKS = 16384
N_WIDE = 32
N_NARROW = 16


def draw_dest(key, part):
    full_key, sender_key = jax.random.split(key)
    full_owner = jax.random.randint(full_key, (N_WIDE,), 0, N_NARROW)
    sender_keys = jax.random.split(sender_key, N_WIDE * N_NARROW)
    full_each = jnp.repeat(full_owner, N_NARROW)

    def one_sender(each_key, favored):
        pick_key, mix_key = jax.random.split(each_key)
        spread = jax.random.permutation(pick_key, (N_NARROW - 1) * SLOT)[:LEAF_DEV - SLOT] // SLOT
        others = (favored + 1 + spread) % N_NARROW
        primary = jnp.zeros((SLOT,), jnp.int32) + favored
        targets = jnp.concatenate([primary, others.astype(jnp.int32)])
        return jax.random.permutation(mix_key, targets)
    return jax.vmap(one_sender)(sender_keys, full_each).reshape(-1).astype(jnp.int32)


def touch_ends(drawn, own_key, low, high):
    longest = drawn.shape.index(max(drawn.shape))
    spots = []
    for shift in (0, 1):
        where = [jax.random.randint(jax.random.fold_in(own_key, axis), (), 0, length) for axis, length in enumerate(drawn.shape)]
        where[longest] = (where[longest] + shift) % drawn.shape[longest]
        spots.append(tuple(where))
    return drawn.at[spots[0]].set(low).at[spots[1]].set(high)


def level_of(key, dims, cuts, least, top_value):
    factor_of, own = 1.0, jax.random.fold_in(key, 6)
    for dim, shards_of in cuts:
        draws = jnp.exp(jax.random.uniform(jax.random.fold_in(own, dim), (shards_of,), jnp.float32, least / len(cuts), top_value / len(cuts)))
        factor_of = factor_of * jnp.repeat(draws, dims[dim] // shards_of).reshape([-1 if axis == dim else 1 for axis in range(len(dims))])
    return factor_of


def gaussian(rng, shape, scale, limit, cuts=(), held_as=jnp.bfloat16):
    values = jax.random.normal(rng, shape, jnp.float32) * scale
    if len(cuts) > 0:
        values = level_of(rng, shape, cuts, -0.22, 0.18) * values
    return jnp.clip(values, min=-limit, max=limit).astype(held_as)


def setup_inputs(seed: int = 0) -> dict:
    key_of = jax.random.split(jax.random.key(seed), 5)
    positions = jnp.clip(jax.random.uniform(key_of[0], (BLOCKS, 3, PART), jnp.float32, -1.0, 1.0) * level_of(key_of[0], (BLOCKS, 3, PART), ((0, 512),), -0.4, 0.0), -1.0, 1.0)
    moments = gaussian(key_of[1], (BLOCKS, 3, PART), 1.0, 6.0, ((0, 512),), jnp.float32)
    counts = touch_ends(jax.random.randint(key_of[2], (BLOCKS,), 1, PART + 1), jax.random.fold_in(key_of[2], 1), 1, PART).astype(jnp.int32)
    dest = draw_dest(jax.random.fold_in(key_of[4], 71), 0)
    return dict(positions=positions, moments=moments, counts=counts, dest=dest)


def exponent_list(order):
    triples = []
    for degree in range(order + 1):
        for power_x in range(degree, -1, -1):
            for power_y in range(degree - power_x, -1, -1):
                triples.append((power_x, power_y, degree - power_x - power_y))
    return triples


def source_tables(order):
    triples = exponent_list(order)
    pick_index = np.zeros((3, len(triples)), np.int32)
    weights = np.zeros((3, len(triples)), np.float32)
    for column, triple in enumerate(triples):
        for axis_id in range(3):
            if triple[axis_id] > 0:
                lowered = list(triple)
                lowered[axis_id] -= 1
                pick_index[axis_id, column] = ((axis_id * order + lowered[2]) * order + lowered[0]) * order + lowered[1]
                weights[axis_id, column] = triple[axis_id] / 16.0
    return pick_index, weights


def shift_table(order):
    triples = exponent_list(order)
    term_count = len(triples)
    table = np.zeros((8 * term_count, term_count), np.float32)
    for octant in range(8):
        sign_list = [2 * ((octant >> axis_id) & 1) - 1 for axis_id in range(3)]
        for column, target_exp in enumerate(triples):
            halving = 0.5 ** sum(target_exp)
            for source_row, source_exp in enumerate(triples):
                if all(source_exp[axis_id] <= target_exp[axis_id] for axis_id in range(3)):
                    entry_value = halving
                    for axis_id in range(3):
                        entry_value *= math.comb(target_exp[axis_id], source_exp[axis_id]) * sign_list[axis_id] ** (target_exp[axis_id] - source_exp[axis_id])
                    table[octant * term_count + source_row, column] = entry_value
    return table


def block_moments(positions, moments, counts, order):
    total_rows = positions.shape[0]
    per_block = positions.shape[2]
    pick_index, weights = source_tables(order)
    weight_rows = jnp.asarray(weights, jnp.float32)
    batch_rows = math.gcd(total_rows, 64)

    def one_batch(batch_in):
        places, dipoles, live_counts = batch_in
        living = (jnp.arange(per_block)[None, :] < live_counts[:, None]).astype(jnp.float32)
        weighted = dipoles * living[:, None, :]

        def powers(coordinate):
            layers = [jnp.ones_like(coordinate)]
            for degree in range(order - 1):
                layers.append(layers[-1] * coordinate)
            return jnp.stack(layers, axis=1)

        along_x = powers(places[:, 0])
        along_y = powers(places[:, 1])
        along_z = powers(places[:, 2])
        planar = (along_x[:, :, None, :] * along_y[:, None, :, :]).reshape(batch_rows, order * order, per_block)
        height = (weighted[:, :, None, :] * along_z[:, None, :, :]).reshape(batch_rows, 3 * order, per_block)
        moment_sums = jnp.einsum("lqp,lrp->lqr", height, planar, precision=lax.Precision.HIGHEST).reshape(batch_rows, -1)
        result = jnp.take(moment_sums, pick_index[0], axis=1) * weight_rows[0][None, :]
        for axis_id in range(1, 3):
            result = result + jnp.take(moment_sums, pick_index[axis_id], axis=1) * weight_rows[axis_id][None, :]
        return result

    batches = (positions.reshape(total_rows // batch_rows, batch_rows, 3, per_block),
               moments.reshape(total_rows // batch_rows, batch_rows, 3, per_block),
               counts.reshape(total_rows // batch_rows, batch_rows))
    return lax.map(one_batch, batches).reshape(total_rows, -1)


def reference(positions, moments, counts, dest):
    translate = jnp.asarray(shift_table(P_SIZE), jnp.float32)
    coef_count = translate.shape[1]
    block_values = block_moments(positions, moments, counts, P_SIZE)
    group_size = LEAF_DEV * N_NARROW
    grouped = dest.reshape(N_WIDE, group_size)
    sequence = (jnp.argsort(grouped, axis=1, stable=True).astype(jnp.int32)
                + (jnp.arange(N_WIDE, dtype=jnp.int32) * group_size)[:, None]).reshape(-1)
    leaves = block_values[sequence]
    owners = jnp.arange(N_NARROW, dtype=jnp.int32)
    tallies = jnp.sum((grouped[:, :, None] == owners[None, None, :]).astype(jnp.int32), axis=1).reshape(-1)
    offsets = jnp.cumsum(tallies).astype(jnp.int32) - tallies
    slot_ids = jnp.arange(OWN_CAP, dtype=jnp.int32)
    leaf_ranks = offsets[:, None] + slot_ids[None, :]
    filled = slot_ids[None, :] < tallies[:, None]
    leaf_out = jnp.where(filled[:, :, None], leaves[jnp.clip(leaf_ranks, 0, BLOCKS - 1)], 0.0)
    partial_value = leaves
    slot_total = OWN_CAP
    pieces = []
    for level_id in range(1, LEVELS + 1):
        pad_rows = (-partial_value.shape[0]) % 8
        partial_value = jnp.concatenate([partial_value, jnp.zeros((pad_rows, coef_count), partial_value.dtype)], axis=0)
        partial_value = jnp.dot(partial_value.reshape(-1, 8 * coef_count), translate, precision=lax.Precision.HIGHEST)
        slot_total = (slot_total + 14) // 8
        box_span = 8 ** level_id
        box_ids = offsets[:, None] // box_span + jnp.arange(slot_total, dtype=jnp.int32)[None, :]
        starts = box_ids * box_span
        owned_box = (starts >= offsets[:, None]) & (starts < (offsets + tallies)[:, None])
        pieces.append(jnp.where(owned_box[:, :, None], partial_value[jnp.clip(box_ids, 0, partial_value.shape[0] - 1)], 0.0))
    box_out = jnp.concatenate(pieces, axis=1).reshape(-1, coef_count)
    return leaf_out.reshape(-1, coef_count), box_out
```

```python
import math

import jax
import jax.numpy as jnp
import numpy as np
from jax import lax
from jax.experimental import pallas as pl
from jax.experimental.pallas import tpu as pltpu
from jax.sharding import PartitionSpec as P

P_SIZE = 10
COEFS = 286
GROUP = 512
F32 = jnp.float32
BF16 = jnp.bfloat16


def exponent_list(order):
    triples = []
    for degree in range(order + 1):
        for power_x in range(degree, -1, -1):
            for power_y in range(degree - power_x, -1, -1):
                triples.append((power_x, power_y, degree - power_x - power_y))
    return triples


def tables():
    triples = exponent_list(P_SIZE)
    shift = np.zeros((256, 384), np.float32)
    for column, target in enumerate(triples):
        for row, source in enumerate(triples[:256]):
            if all(s <= t for s, t in zip(source, target)):
                shift[row, column] = 0.5 ** sum(target) * math.prod(
                    math.comb(t, s) for s, t in zip(source, target)
                )
    signs = np.ones((8, 384), np.float32)
    for octant in range(8):
        for column, target in enumerate(triples):
            for axis in range(3):
                if not (octant >> axis) & 1 and target[axis] % 2:
                    signs[octant, column] = -signs[octant, column]
    return shift, signs


def split(value):
    high = value.astype(BF16)
    return high, (value - high.astype(F32)).astype(BF16)


def moments_kernel(places_ref, dipoles_ref, counts_ref, dest_ref, out_ref, grid_ref, sums_ref):
    index_of = {triple: i for i, triple in enumerate(exponent_list(P_SIZE))}

    def turned(values):
        quarters = [values[:, 64 * q : 64 * q + 64] for q in range(4)]
        return jnp.concatenate(quarters, axis=0).T

    live = jnp.concatenate([counts_ref[...]] * 4, axis=1)
    rows = lax.broadcasted_iota(jnp.int32, (64, 128), 0)
    lanes = lax.broadcasted_iota(jnp.int32, (64, 128), 1)
    living = rows + 64 * (lanes // 32) < live
    for axis in range(3):
        grid_ref[axis] = turned(places_ref[axis])
        grid_ref[3 + axis] = jnp.where(living, turned(dipoles_ref[axis]), 0.0)
    sums_ref[...] = jnp.zeros(sums_ref.shape, F32)

    def half(step, carry):
        picked = pl.ds(pl.multiple_of(step * 32, 32), 32)
        x, y, z, mx, my, mz = [grid_ref[k, picked, :] for k in range(6)]

        def note(triple, psi):
            folded = (psi[0:8] + psi[8:16]) + (psi[16:24] + psi[24:32])
            sums_ref[index_of[triple]] += folded

        phi_x, psi_x = None, None
        for a in range(P_SIZE + 1):
            if a == 1:
                phi_x, psi_x = x, mx
            elif a > 1:
                phi_x, psi_x = phi_x * x, psi_x * x + mx * phi_x
            phi_y, psi_y = phi_x, psi_x
            for e in range(P_SIZE + 1 - a):
                if e > 0:
                    if phi_y is None:
                        phi_y, psi_y = y, my
                    elif psi_y is None:
                        phi_y, psi_y = phi_y * y, my * phi_y
                    else:
                        phi_y, psi_y = phi_y * y, psi_y * y + my * phi_y
                phi, psi = phi_y, psi_y
                for c in range(P_SIZE + 1 - a - e):
                    if c > 0:
                        if phi is None:
                            phi, psi = z, mz
                        else:
                            phi, psi = phi * z, psi * z + mz * phi
                    if psi is not None:
                        note((a, e, c), psi)
        return carry

    lax.fori_loop(0, 2, half, 0)
    folded = jnp.sum(sums_ref[...], axis=1)
    blank = jnp.zeros((1, 96), F32)
    where_to = jnp.concatenate([dest_ref[...].astype(F32), blank], axis=1)
    row = lax.broadcasted_iota(jnp.int32, folded.shape, 0)
    folded = jnp.where(row == COEFS, where_to, folded * (1.0 / 16.0))
    folded = jnp.concatenate([folded, jnp.zeros((96, 128), F32)], axis=0).T
    values = (folded[0:32] + folded[32:64]) + (folded[64:96] + folded[96:128])
    out_ref[0:32] = values[:, 0:128]
    out_ref[32:64] = values[:, 128:256]
    tail = values[:, 256:288]
    out_ref[64:72] = jnp.concatenate([tail[8 * g : 8 * g + 8] for g in range(4)], axis=1)


def tree_kernel(
    where_ref, got_ref, shift_ref, signs_ref, leaf_ref, box_ref, send_ref, own_ref
):
    me = where_ref[0]
    group = where_ref[1]
    lane = lax.broadcasted_iota(jnp.int32, (128, 128), 1)
    tails = got_ref[:, 64:72, :].reshape(128, 128)
    turned = tails.T
    dest_row = jnp.concatenate([turned[32 * g + 30 : 32 * g + 31] for g in range(4)], axis=1)
    spot = lax.broadcasted_iota(jnp.int32, (1, GROUP), 1)
    block_row = ((spot // 8) % 16) * 32 + (spot // 128) * 8 + spot % 8
    key_row = dest_row * 512.0 + block_row.astype(F32)
    spot = lax.broadcasted_iota(jnp.int32, (128, 1), 0)
    high_parts, low_parts, pair_parts, key_parts = [], [], [], []
    for g in range(4):
        tail = tails if g == 0 else pltpu.roll(tails, 128 - 32 * g, 1)
        block = (spot // 8) * 32 + g * 8 + spot % 8
        key_parts.append(tail[:, 30:31] * 512.0 + block.astype(F32))
        first = got_ref[:, 8 * g : 8 * g + 8, :].reshape(128, 128)
        second = got_ref[:, 32 + 8 * g : 40 + 8 * g, :].reshape(128, 128)
        tail = jnp.where(lane < 30, tail, 0.0)
        top = tail.astype(BF16).astype(F32)
        pair = top + pltpu.roll(tail - top, 32, 1)
        (first_high, first_low), (second_high, second_low) = split(first), split(second)
        high_parts.append(jnp.concatenate([first_high, second_high], axis=1))
        low_parts.append(jnp.concatenate([first_low, second_low], axis=1))
        pair_parts.append(pair.astype(BF16))
    held = jnp.concatenate(
        [
            jnp.concatenate(high_parts, axis=0),
            jnp.concatenate(low_parts, axis=0),
            jnp.concatenate(pair_parts, axis=0),
        ],
        axis=1,
    )
    smaller = jnp.zeros((8, GROUP), F32)
    for g in range(4):
        less = jnp.where(key_parts[g] < key_row, 1.0, 0.0)
        smaller = smaller + jnp.sum(less.reshape(16, 8, GROUP), axis=0)
    rank = jnp.sum(smaller, axis=0, keepdims=True).astype(jnp.int32)
    mine = me.astype(F32)
    start = jnp.sum(jnp.where(dest_row < mine, 1.0, 0.0), axis=1, keepdims=True).astype(jnp.int32)
    tally = jnp.sum(jnp.where(dest_row == mine, 1.0, 0.0), axis=1, keepdims=True).astype(jnp.int32)
    row = lax.broadcasted_iota(jnp.int32, (GROUP, 1), 0)
    turned_row = (row % 8) * 64 + ((row // 8) % 8) * 8 + row // 64
    slot = lax.broadcasted_iota(jnp.int32, (128, 1), 0)
    wanted = jnp.concatenate([turned_row, jnp.where(slot < tally, start + slot, -1)], axis=0)
    chosen = jnp.where(wanted == rank, 1.0, 0.0).astype(BF16)
    placed = jnp.dot(chosen, held, preferred_element_type=F32)
    own = placed[GROUP:]
    leaf_first = (own[:, 0:128] + own[:, 256:384]).T
    leaf_second = (own[:, 128:256] + own[:, 384:512]).T
    own_tail = own[:, 512:640]
    leaf_tail = (own_tail + pltpu.roll(own_tail, 96, 1)).T
    leaf_ref[0:128] = leaf_first
    leaf_ref[128:256] = leaf_second
    leaf_ref[256:COEFS] = leaf_tail[0 : COEFS - 256]

    shift = shift_ref[...]
    tiny = 2.0**-P_SIZE

    def moved(high, low):
        stacked = jnp.dot(
            jnp.concatenate([high, low], axis=0), shift, preferred_element_type=F32
        )
        count = high.shape[0]
        return stacked[:count] + stacked[count:]

    def signed(octant):
        return signs_ref[octant : octant + 1, :]

    sign_rows = jnp.concatenate(
        [jnp.broadcast_to(signed(o)[:, 0:256], (64, 256)) for o in range(8)], axis=0
    )
    sons = placed[:GROUP]
    high = (sons[:, 0:256] * sign_rows).astype(BF16)
    low = (sons[:, 256:512] * sign_rows).astype(BF16)
    parts = moved(high, low)
    level = parts[0:64] * signed(0)
    tail_sum = sons[0:64, 512:640]
    for o in range(1, 8):
        level = level + parts[64 * o : 64 * o + 64] * signed(o)
        tail_sum = tail_sum + sons[64 * o : 64 * o + 64, 512:640]
    tail_lane = lax.broadcasted_iota(jnp.int32, (1, 128), 1) < 30

    def with_tail(body, tail):
        added = body[:, 256:384] + jnp.where(tail_lane, tail * tiny, 0.0)
        return jnp.concatenate([body[:, 0:256], added], axis=1)

    level_1 = with_tail(level, tail_sum + pltpu.roll(tail_sum, 96, 1))
    sign_rows = jnp.concatenate(
        [jnp.broadcast_to(signed(o), (8, 384)) for o in range(8)], axis=0
    )
    parts = moved(*split(level_1[:, 0:256] * sign_rows[:, 0:256])) * sign_rows
    level = jnp.sum(parts.reshape(8, 8, 384), axis=0)
    tail_sum = jnp.sum(level_1[:, 256:384].reshape(8, 8, 128), axis=0)
    level_2 = with_tail(level, tail_sum)
    all_signs = signs_ref[...]
    parts = moved(*split(level_2[:, 0:256] * all_signs[:, 0:256])) * all_signs
    level = jnp.sum(parts, axis=0, keepdims=True)
    tail_sum = jnp.sum(level_2[:, 256:384], axis=0, keepdims=True)
    level_3 = with_tail(level, tail_sum)
    sublane = lax.broadcasted_iota(jnp.int32, (8, 384), 0)

    def share(value, octant):
        sign = jnp.sum(jnp.where(sublane == octant, all_signs, 0.0), axis=0, keepdims=True)
        eight = jnp.broadcast_to(value * sign, (8, 384))
        part = moved(*split(eight[:, 0:256]))[0:1] * sign
        return with_tail(part, value[:, 256:384])

    level_4 = share(level_3, group % 8)
    level_5 = share(level_4, group // 8)
    send_ref[0:1] = level_4[:, 0:128]
    send_ref[1:2] = level_4[:, 128:256]
    send_ref[2:3] = level_4[:, 256:384]
    send_ref[3:4] = level_5[:, 0:128]
    send_ref[4:5] = level_5[:, 128:256]
    send_ref[5:6] = level_5[:, 256:384]
    send_ref[6:8] = jnp.zeros((2, 128), F32)

    boxes = jnp.concatenate(
        [level_1, level_2, level_3, jnp.zeros((55, 384), F32)], axis=0
    )
    end = start + tally
    out_slot = lax.broadcasted_iota(jnp.int32, (32, 1), 0)
    box_1 = start // 8 + out_slot
    box_2 = start // 64 + out_slot - 17
    source = jnp.where((box_1 * 8 >= start) & (box_1 * 8 < end), (box_1 % 8) * 8 + box_1 // 8, -1)
    source_2 = jnp.where((box_2 * 64 >= start) & (box_2 * 64 < end), 64 + box_2, -1)
    first_of_group = (start == 0) & (tally > 0)
    source_3 = jnp.where(first_of_group & (out_slot == 20), 72, -1)
    source = jnp.where(out_slot < 17, source, jnp.where(out_slot < 20, source_2, source_3))
    column = lax.broadcasted_iota(jnp.int32, (32, 128), 1)
    select = jnp.where(column == source, 1.0, 0.0).astype(BF16)
    high, low = split(boxes)
    picked = jnp.dot(select, high, preferred_element_type=F32) + jnp.dot(
        select, low, preferred_element_type=F32
    )
    box_ref[...] = picked[0:26, 0:COEFS]
    heads = first_of_group & (lax.broadcasted_iota(jnp.int32, (8, 128), 0) >= 0)
    own_ref[...] = jnp.where(heads, 1.0, 0.0)


def finish_kernel(where_ref, own_ref, four_ref, five_ref, part_ref, box_ref):
    group = where_ref[1]
    own = own_ref[0:1]
    keep_4 = own * jnp.where(group % 8 == 0, 1.0, 0.0)
    keep_5 = own * jnp.where(group == 0, 1.0, 0.0)
    box_ref[...] = part_ref[...]
    for at, keep, ref, base in ((22, keep_4, four_ref, 0), (24, keep_5, five_ref, 3)):
        box_ref[at : at + 1, 0:128] = ref[base : base + 1] * keep
        box_ref[at : at + 1, 128:256] = ref[base + 1 : base + 2] * keep
        last = ref[base + 2 : base + 3] * keep
        box_ref[at : at + 1, 256:COEFS] = last[:, 0 : COEFS - 256]


VMEM = pl.BlockSpec(memory_space=pltpu.VMEM)
SMEM = pl.BlockSpec(memory_space=pltpu.SMEM)
PARAMS = pltpu.CompilerParams(vmem_limit_bytes=40 * 1024 * 1024)


def shards(positions, moments, counts, dest):
    shift, signs = tables()
    where = jnp.stack([lax.axis_index("narrow"), lax.axis_index("wide")]).astype(jnp.int32)
    sent = pl.pallas_call(
        moments_kernel,
        out_shape=jax.ShapeDtypeStruct((72, 128), F32),
        in_specs=[VMEM] * 4,
        out_specs=VMEM,
        scratch_shapes=[pltpu.VMEM((6, 64, 128), F32), pltpu.VMEM((288, 8, 128), F32)],
        compiler_params=PARAMS,
    )(
        jnp.transpose(positions, (1, 0, 2)),
        jnp.transpose(moments, (1, 0, 2)),
        counts.reshape(1, 32),
        dest.reshape(1, 32),
    )
    got = lax.all_to_all(
        jnp.broadcast_to(sent[None], (16, 72, 128)), "narrow", split_axis=0, concat_axis=0, tiled=True
    )
    leaf, box, share, own = pl.pallas_call(
        tree_kernel,
        out_shape=(
            jax.ShapeDtypeStruct((COEFS, 128), F32),
            jax.ShapeDtypeStruct((26, COEFS), F32),
            jax.ShapeDtypeStruct((8, 128), F32),
            jax.ShapeDtypeStruct((8, 128), F32),
        ),
        in_specs=[SMEM, VMEM, VMEM, VMEM],
        out_specs=(VMEM,) * 4,
        compiler_params=PARAMS,
    )(where, got, jnp.asarray(shift, BF16), jnp.asarray(signs, F32))
    pair = share + lax.ppermute(share, "wide", [(2 * i + 1, 2 * i) for i in range(16)])
    quad = pair
    for j in (2, 4, 6):
        quad = quad + lax.ppermute(pair, "wide", [(8 * q + j, 8 * q) for q in range(4)])
    top = quad
    for j in (24, 16, 8):
        top = top + lax.ppermute(quad, "wide", [(j, 0)])
    box = pl.pallas_call(
        finish_kernel,
        out_shape=jax.ShapeDtypeStruct((26, COEFS), F32),
        in_specs=[SMEM, VMEM, VMEM, VMEM, VMEM],
        out_specs=VMEM,
        compiler_params=PARAMS,
    )(where, own, quad, top, box)
    return leaf.T, box


def solution(mesh):
    both = ("wide", "narrow")
    placed = (P(both, None, None), P(both, None, None), P(both), P(both))
    return jax.shard_map(
        shards,
        mesh=mesh,
        in_specs=placed,
        out_specs=(P(both, None), P(both, None)),
        check_vma=False,
    )
```

```python
import math

import jax
import jax.numpy as jnp
import numpy as np
from jax import lax
from jax.experimental import pallas as pl
from jax.experimental.pallas import tpu as pltpu
from jax.sharding import PartitionSpec as P

P_SIZE = 10
COEFS = 286
GROUP = 512
F32 = jnp.float32
BF16 = jnp.bfloat16


def exponent_list(order):
    triples = []
    for degree in range(order + 1):
        for power_x in range(degree, -1, -1):
            for power_y in range(degree - power_x, -1, -1):
                triples.append((power_x, power_y, degree - power_x - power_y))
    return triples


def tables():
    triples = exponent_list(P_SIZE)
    shift = np.zeros((256, 384), np.float32)
    for column, target in enumerate(triples):
        for row, source in enumerate(triples[:256]):
            if all(s <= t for s, t in zip(source, target)):
                shift[row, column] = 0.5 ** sum(target) * math.prod(
                    math.comb(t, s) for s, t in zip(source, target)
                )
    signs = np.ones((8, 384), np.float32)
    for octant in range(8):
        for column, target in enumerate(triples):
            for axis in range(3):
                if not (octant >> axis) & 1 and target[axis] % 2:
                    signs[octant, column] = -signs[octant, column]
    return shift, signs


def split(value):
    high = value.astype(BF16)
    return high, (value - high.astype(F32)).astype(BF16)


def moments_kernel(
    places_hbm, dipoles_hbm, counts_hbm, dest_hbm, out_hbm,
    places_ref, dipoles_ref, counts_ref, dest_ref, out_ref, grid_ref, sums_ref, in_sems, out_sem,
):
    pairs = (
        (places_hbm, places_ref),
        (dipoles_hbm, dipoles_ref),
        (counts_hbm, counts_ref),
        (dest_hbm, dest_ref),
    )
    copies = [pltpu.make_async_copy(a, b, in_sems.at[k]) for k, (a, b) in enumerate(pairs)]
    for copy in copies:
        copy.start()
    sums_ref[...] = jnp.zeros(sums_ref.shape, F32)
    for copy in copies:
        copy.wait()
    index_of = {triple: i for i, triple in enumerate(exponent_list(P_SIZE))}

    def turned(values):
        quarters = [values[:, 64 * q : 64 * q + 64] for q in range(4)]
        return jnp.concatenate(quarters, axis=0).T

    live = jnp.concatenate([counts_ref[...]] * 4, axis=1)
    rows = lax.broadcasted_iota(jnp.int32, (64, 128), 0)
    lanes = lax.broadcasted_iota(jnp.int32, (64, 128), 1)
    living = rows + 64 * (lanes // 32) < live
    for axis in range(3):
        grid_ref[axis] = turned(places_ref[axis])
        grid_ref[3 + axis] = jnp.where(living, turned(dipoles_ref[axis]), 0.0)

    def half(step, carry):
        picked = pl.ds(pl.multiple_of(step * 32, 32), 32)
        x, y, z, mx, my, mz = [grid_ref[k, picked, :] for k in range(6)]

        def note(triple, psi):
            folded = (psi[0:8] + psi[8:16]) + (psi[16:24] + psi[24:32])
            sums_ref[index_of[triple]] += folded

        phi_x, psi_x = None, None
        for a in range(P_SIZE + 1):
            if a == 1:
                phi_x, psi_x = x, mx
            elif a > 1:
                phi_x, psi_x = phi_x * x, psi_x * x + mx * phi_x
            phi_y, psi_y = phi_x, psi_x
            for e in range(P_SIZE + 1 - a):
                if e > 0:
                    if phi_y is None:
                        phi_y, psi_y = y, my
                    elif psi_y is None:
                        phi_y, psi_y = phi_y * y, my * phi_y
                    else:
                        phi_y, psi_y = phi_y * y, psi_y * y + my * phi_y
                phi, psi = phi_y, psi_y
                for c in range(P_SIZE + 1 - a - e):
                    if c > 0:
                        if phi is None:
                            phi, psi = z, mz
                        else:
                            phi, psi = phi * z, psi * z + mz * phi
                    if psi is not None:
                        note((a, e, c), psi)
        return carry

    lax.fori_loop(0, 2, half, 0)
    folded = jnp.sum(sums_ref[...], axis=1)
    blank = jnp.zeros((1, 96), F32)
    where_to = jnp.concatenate([dest_ref[...].astype(F32), blank], axis=1)
    row = lax.broadcasted_iota(jnp.int32, folded.shape, 0)
    folded = jnp.where(row == COEFS, where_to, folded * (1.0 / 16.0))
    folded = jnp.concatenate([folded, jnp.zeros((96, 128), F32)], axis=0).T
    values = (folded[0:32] + folded[32:64]) + (folded[64:96] + folded[96:128])
    out_ref[0:32] = values[:, 0:128]
    out_ref[32:64] = values[:, 128:256]
    tail = values[:, 256:288]
    out_ref[64:72] = jnp.concatenate([tail[8 * g : 8 * g + 8] for g in range(4)], axis=1)
    copies = [pltpu.make_async_copy(out_ref, out_hbm.at[n], out_sem.at[n]) for n in range(16)]
    for copy in copies:
        copy.start()
    for copy in copies:
        copy.wait()


def tree_kernel(
    where_ref, got_ref, shift_ref, signs_ref, leaf_ref, box_ref, send_ref, own_ref
):
    me = where_ref[0]
    group = where_ref[1]
    lane = lax.broadcasted_iota(jnp.int32, (128, 128), 1)
    tails = got_ref[:, 64:72, :].reshape(128, 128)
    turned = tails.T
    dest_row = jnp.concatenate([turned[32 * g + 30 : 32 * g + 31] for g in range(4)], axis=1)
    spot = lax.broadcasted_iota(jnp.int32, (1, GROUP), 1)
    block_row = ((spot // 8) % 16) * 32 + (spot // 128) * 8 + spot % 8
    key_row = dest_row * 512.0 + block_row.astype(F32)
    spot = lax.broadcasted_iota(jnp.int32, (128, 1), 0)
    high_parts, low_parts, pair_parts, key_parts = [], [], [], []
    for g in range(4):
        tail = tails if g == 0 else pltpu.roll(tails, 128 - 32 * g, 1)
        block = (spot // 8) * 32 + g * 8 + spot % 8
        key_parts.append(tail[:, 30:31] * 512.0 + block.astype(F32))
        first = got_ref[:, 8 * g : 8 * g + 8, :].reshape(128, 128)
        second = got_ref[:, 32 + 8 * g : 40 + 8 * g, :].reshape(128, 128)
        tail = jnp.where(lane < 30, tail, 0.0)
        top = tail.astype(BF16).astype(F32)
        pair = top + pltpu.roll(tail - top, 32, 1)
        (first_high, first_low), (second_high, second_low) = split(first), split(second)
        high_parts.append(jnp.concatenate([first_high, second_high], axis=1))
        low_parts.append(jnp.concatenate([first_low, second_low], axis=1))
        pair_parts.append(pair.astype(BF16))
    held = jnp.concatenate(
        [
            jnp.concatenate(high_parts, axis=0),
            jnp.concatenate(low_parts, axis=0),
            jnp.concatenate(pair_parts, axis=0),
        ],
        axis=1,
    )
    smaller = jnp.zeros((8, GROUP), F32)
    for g in range(4):
        less = jnp.where(key_parts[g] < key_row, 1.0, 0.0)
        smaller = smaller + jnp.sum(less.reshape(16, 8, GROUP), axis=0)
    rank = jnp.sum(smaller, axis=0, keepdims=True).astype(jnp.int32)
    mine = me.astype(F32)
    start = jnp.sum(jnp.where(dest_row < mine, 1.0, 0.0), axis=1, keepdims=True).astype(jnp.int32)
    tally = jnp.sum(jnp.where(dest_row == mine, 1.0, 0.0), axis=1, keepdims=True).astype(jnp.int32)
    row = lax.broadcasted_iota(jnp.int32, (GROUP, 1), 0)
    turned_row = (row % 8) * 64 + ((row // 8) % 8) * 8 + row // 64
    slot = lax.broadcasted_iota(jnp.int32, (128, 1), 0)
    wanted = jnp.concatenate([turned_row, jnp.where(slot < tally, start + slot, -1)], axis=0)
    chosen = jnp.where(wanted == rank, 1.0, 0.0).astype(BF16)
    placed = jnp.dot(chosen, held, preferred_element_type=F32)
    own = placed[GROUP:]
    leaf_first = (own[:, 0:128] + own[:, 256:384]).T
    leaf_second = (own[:, 128:256] + own[:, 384:512]).T
    own_tail = own[:, 512:640]
    leaf_tail = (own_tail + pltpu.roll(own_tail, 96, 1)).T
    leaf_ref[0:128] = leaf_first
    leaf_ref[128:256] = leaf_second
    leaf_ref[256:COEFS] = leaf_tail[0 : COEFS - 256]

    shift = shift_ref[...]
    tiny = 2.0**-P_SIZE

    def moved(high, low):
        stacked = jnp.dot(
            jnp.concatenate([high, low], axis=0), shift, preferred_element_type=F32
        )
        count = high.shape[0]
        return stacked[:count] + stacked[count:]

    def signed(octant):
        return signs_ref[octant : octant + 1, :]

    sign_rows = jnp.concatenate(
        [jnp.broadcast_to(signed(o)[:, 0:256], (64, 256)) for o in range(8)], axis=0
    )
    sons = placed[:GROUP]
    high = (sons[:, 0:256] * sign_rows).astype(BF16)
    low = (sons[:, 256:512] * sign_rows).astype(BF16)
    parts = moved(high, low)
    level = parts[0:64] * signed(0)
    tail_sum = sons[0:64, 512:640]
    for o in range(1, 8):
        level = level + parts[64 * o : 64 * o + 64] * signed(o)
        tail_sum = tail_sum + sons[64 * o : 64 * o + 64, 512:640]
    tail_lane = lax.broadcasted_iota(jnp.int32, (1, 128), 1) < 30

    def with_tail(body, tail):
        added = body[:, 256:384] + jnp.where(tail_lane, tail * tiny, 0.0)
        return jnp.concatenate([body[:, 0:256], added], axis=1)

    level_1 = with_tail(level, tail_sum + pltpu.roll(tail_sum, 96, 1))
    sign_rows = jnp.concatenate(
        [jnp.broadcast_to(signed(o), (8, 384)) for o in range(8)], axis=0
    )
    parts = moved(*split(level_1[:, 0:256] * sign_rows[:, 0:256])) * sign_rows
    level = jnp.sum(parts.reshape(8, 8, 384), axis=0)
    tail_sum = jnp.sum(level_1[:, 256:384].reshape(8, 8, 128), axis=0)
    level_2 = with_tail(level, tail_sum)
    all_signs = signs_ref[...]
    parts = moved(*split(level_2[:, 0:256] * all_signs[:, 0:256])) * all_signs
    level = jnp.sum(parts, axis=0, keepdims=True)
    tail_sum = jnp.sum(level_2[:, 256:384], axis=0, keepdims=True)
    level_3 = with_tail(level, tail_sum)
    sublane = lax.broadcasted_iota(jnp.int32, (8, 384), 0)

    def share(value, octant):
        sign = jnp.sum(jnp.where(sublane == octant, all_signs, 0.0), axis=0, keepdims=True)
        eight = jnp.broadcast_to(value * sign, (8, 384))
        part = moved(*split(eight[:, 0:256]))[0:1] * sign
        return with_tail(part, value[:, 256:384])

    level_4 = share(level_3, group % 8)
    level_5 = share(level_4, group // 8)
    send_ref[0:1] = level_4[:, 0:128]
    send_ref[1:2] = level_4[:, 128:256]
    send_ref[2:3] = level_4[:, 256:384]
    send_ref[3:4] = level_5[:, 0:128]
    send_ref[4:5] = level_5[:, 128:256]
    send_ref[5:6] = level_5[:, 256:384]
    send_ref[6:8] = jnp.zeros((2, 128), F32)

    boxes = jnp.concatenate(
        [level_1, level_2, level_3, jnp.zeros((55, 384), F32)], axis=0
    )
    end = start + tally
    out_slot = lax.broadcasted_iota(jnp.int32, (32, 1), 0)
    box_1 = start // 8 + out_slot
    box_2 = start // 64 + out_slot - 17
    source = jnp.where((box_1 * 8 >= start) & (box_1 * 8 < end), (box_1 % 8) * 8 + box_1 // 8, -1)
    source_2 = jnp.where((box_2 * 64 >= start) & (box_2 * 64 < end), 64 + box_2, -1)
    first_of_group = (start == 0) & (tally > 0)
    source_3 = jnp.where(first_of_group & (out_slot == 20), 72, -1)
    source = jnp.where(out_slot < 17, source, jnp.where(out_slot < 20, source_2, source_3))
    column = lax.broadcasted_iota(jnp.int32, (32, 128), 1)
    select = jnp.where(column == source, 1.0, 0.0).astype(BF16)
    high, low = split(boxes)
    picked = jnp.dot(select, high, preferred_element_type=F32) + jnp.dot(
        select, low, preferred_element_type=F32
    )
    box_ref[...] = picked[0:26, 0:COEFS]
    heads = first_of_group & (lax.broadcasted_iota(jnp.int32, (8, 128), 0) >= 0)
    own_ref[...] = jnp.where(heads, 1.0, 0.0)


def finish_kernel(where_ref, own_ref, four_ref, five_ref, part_ref, box_ref):
    group = where_ref[1]
    own = own_ref[0:1]
    keep_4 = own * jnp.where(group % 8 == 0, 1.0, 0.0)
    keep_5 = own * jnp.where(group == 0, 1.0, 0.0)
    box_ref[...] = part_ref[...]
    for at, keep, ref, base in ((22, keep_4, four_ref, 0), (24, keep_5, five_ref, 3)):
        box_ref[at : at + 1, 0:128] = ref[base : base + 1] * keep
        box_ref[at : at + 1, 128:256] = ref[base + 1 : base + 2] * keep
        last = ref[base + 2 : base + 3] * keep
        box_ref[at : at + 1, 256:COEFS] = last[:, 0 : COEFS - 256]


def permute(value, *pairs):
    return lax.ppermute(value, "wide", list(pairs))


def across(share):
    four = permute(share, *((8 + i, i) for i in range(4)))
    pair = share + permute(share, *((2 * i + 1, 2 * i) for i in range(16)))
    eight = permute(pair, (16, 0), (18, 1))
    ten = permute(pair, (20, 0), (22, 1))
    twelve = permute(pair, (24, 0), (26, 1))
    six = permute(pair, (12, 0), (14, 1))
    after, four = lax.optimization_barrier((pair, four))
    fourteen = permute(after, (28, 0), (30, 1))
    row = lax.broadcasted_iota(jnp.int32, (8, 128), 0)
    mixed = share + jnp.where(row < 3, 0.0, four)
    quads = [[8 * q + j for j in range(8)] for q in range(4)]
    spread = jnp.broadcast_to(mixed[None], (8, 8, 128))
    quad = jnp.sum(
        lax.all_to_all(spread, "wide", 0, 0, axis_index_groups=quads, tiled=True), axis=0
    )
    late = eight + ten + twelve + six + fourteen
    return quad, quad + late + permute(late, (1, 0))


VMEM = pl.BlockSpec(memory_space=pltpu.VMEM)
HBM = pl.BlockSpec(memory_space=pltpu.HBM)
SMEM = pl.BlockSpec(memory_space=pltpu.SMEM)
PARAMS = pltpu.CompilerParams(vmem_limit_bytes=40 * 1024 * 1024)


def shards(positions, moments, counts, dest):
    shift, signs = tables()
    where = jnp.stack([lax.axis_index("narrow"), lax.axis_index("wide")]).astype(jnp.int32)
    sent = pl.pallas_call(
        moments_kernel,
        out_shape=jax.ShapeDtypeStruct((16, 72, 128), F32),
        in_specs=[HBM] * 4,
        out_specs=HBM,
        scratch_shapes=[
            pltpu.VMEM((3, 32, 256), F32),
            pltpu.VMEM((3, 32, 256), F32),
            pltpu.VMEM((1, 32), jnp.int32),
            pltpu.VMEM((1, 32), jnp.int32),
            pltpu.VMEM((72, 128), F32),
            pltpu.VMEM((6, 64, 128), F32),
            pltpu.VMEM((288, 8, 128), F32),
            pltpu.SemaphoreType.DMA((4,)),
            pltpu.SemaphoreType.DMA((16,)),
        ],
        compiler_params=pltpu.CompilerParams(vmem_limit_bytes=64 * 1024 * 1024 - 65536),
    )(
        jnp.transpose(positions, (1, 0, 2)),
        jnp.transpose(moments, (1, 0, 2)),
        counts.reshape(1, 32),
        dest.reshape(1, 32),
    )
    got = lax.all_to_all(sent, "narrow", split_axis=0, concat_axis=0, tiled=True)
    leaf, box, share, own = pl.pallas_call(
        tree_kernel,
        out_shape=(
            jax.ShapeDtypeStruct((COEFS, 128), F32),
            jax.ShapeDtypeStruct((26, COEFS), F32),
            jax.ShapeDtypeStruct((8, 128), F32),
            jax.ShapeDtypeStruct((8, 128), F32),
        ),
        in_specs=[SMEM, VMEM, VMEM, VMEM],
        out_specs=(VMEM,) * 4,
        compiler_params=PARAMS,
    )(where, got, jnp.asarray(shift, BF16), jnp.asarray(signs, F32))
    quad, top = across(share)
    box = pl.pallas_call(
        finish_kernel,
        out_shape=jax.ShapeDtypeStruct((26, COEFS), F32),
        in_specs=[SMEM, VMEM, VMEM, VMEM, VMEM],
        out_specs=VMEM,
        compiler_params=PARAMS,
    )(where, own, quad, top, box)
    return leaf.T, box


def solution(mesh):
    both = ("wide", "narrow")
    placed = (P(both, None, None), P(both, None, None), P(both), P(both))
    return jax.shard_map(
        shards,
        mesh=mesh,
        in_specs=placed,
        out_specs=(P(both, None), P(both, None)),
        check_vma=False,
    )
```

```python
import math

import jax
import jax.numpy as jnp
import numpy as np
from jax import lax
from jax.experimental import pallas as pl
from jax.experimental.pallas import tpu as pltpu
from jax.sharding import PartitionSpec as P

P_SIZE = 10
COEFS = 286
GROUP = 512
F32 = jnp.float32
BF16 = jnp.bfloat16


def exponent_list(order):
    triples = []
    for degree in range(order + 1):
        for power_x in range(degree, -1, -1):
            for power_y in range(degree - power_x, -1, -1):
                triples.append((power_x, power_y, degree - power_x - power_y))
    return triples


def tables():
    triples = exponent_list(P_SIZE)
    shift = np.zeros((256, 384), np.float32)
    for column, target in enumerate(triples):
        for row, source in enumerate(triples[:256]):
            if all(s <= t for s, t in zip(source, target)):
                shift[row, column] = 0.5 ** sum(target) * math.prod(
                    math.comb(t, s) for s, t in zip(source, target)
                )
    signs = np.ones((8, 384), np.float32)
    for octant in range(8):
        for column, target in enumerate(triples):
            for axis in range(3):
                if not (octant >> axis) & 1 and target[axis] % 2:
                    signs[octant, column] = -signs[octant, column]
    return shift, signs


def split(value):
    high = value.astype(BF16)
    return high, (value - high.astype(F32)).astype(BF16)


def moments_kernel(
    places_hbm, dipoles_hbm, counts_hbm, dest_hbm, out_hbm,
    places_ref, dipoles_ref, counts_ref, dest_ref, out_ref, grid_ref, sums_ref, in_sems, out_sem,
):
    pairs = [(counts_hbm, counts_ref), (dest_hbm, dest_ref)]
    for axis in range(3):
        pairs.append((places_hbm.at[axis], places_ref.at[axis]))
        pairs.append((dipoles_hbm.at[axis], dipoles_ref.at[axis]))
    copies = [pltpu.make_async_copy(a, b, in_sems.at[k]) for k, (a, b) in enumerate(pairs)]
    for copy in copies:
        copy.start()
    sums_ref[...] = jnp.zeros(sums_ref.shape, F32)
    for copy in copies:
        copy.wait()
    index_of = {triple: i for i, triple in enumerate(exponent_list(P_SIZE))}

    def turned(values):
        quarters = [values[:, 64 * q : 64 * q + 64] for q in range(4)]
        return jnp.concatenate(quarters, axis=0).T

    live = jnp.concatenate([counts_ref[...]] * 4, axis=1)
    rows = lax.broadcasted_iota(jnp.int32, (64, 128), 0)
    lanes = lax.broadcasted_iota(jnp.int32, (64, 128), 1)
    living = rows + 64 * (lanes // 32) < live
    for axis in range(3):
        grid_ref[axis] = turned(places_ref[axis])
        grid_ref[3 + axis] = jnp.where(living, turned(dipoles_ref[axis]), 0.0)

    def stripe(step, carry):
        picked = pl.ds(pl.multiple_of(step * 32, 32), 32)
        x, y, z, mx, my, mz = [grid_ref[k, picked, :] for k in range(6)]

        def note(triple, psi):
            folded = (psi[0:8] + psi[8:16]) + (psi[16:24] + psi[24:32])
            sums_ref[index_of[triple]] += folded

        phi_x, psi_x = None, None
        for a in range(P_SIZE + 1):
            if a == 1:
                phi_x, psi_x = x, mx
            elif a > 1:
                phi_x, psi_x = phi_x * x, psi_x * x + mx * phi_x
            phi, psi = phi_x, psi_x
            for e in range(P_SIZE + 1 - a):
                if e > 0:
                    if phi is None:
                        phi, psi = y, my
                    else:
                        phi, psi = phi * y, psi * y + my * phi
                if psi is not None:
                    note((a, e, 0), psi)
                deep, omega = psi, mz if phi is None else mz * phi
                for c in range(1, P_SIZE + 1 - a - e):
                    deep = omega if deep is None else deep * z + omega
                    note((a, e, c), deep)
                    omega = omega * z
        return carry

    lax.fori_loop(0, 2, stripe, 0)
    folded = jnp.sum(sums_ref[...], axis=1)
    blank = jnp.zeros((1, 96), F32)
    where_to = jnp.concatenate([dest_ref[...].astype(F32), blank], axis=1)
    row = lax.broadcasted_iota(jnp.int32, folded.shape, 0)
    folded = jnp.where(row == COEFS, where_to, folded * (1.0 / 16.0))
    folded = jnp.concatenate([folded, jnp.zeros((96, 128), F32)], axis=0).T
    values = (folded[0:32] + folded[32:64]) + (folded[64:96] + folded[96:128])
    out_ref[0:32] = values[:, 0:128]
    out_ref[32:64] = values[:, 128:256]
    tail = values[:, 256:288]
    out_ref[64:72] = jnp.concatenate([tail[8 * g : 8 * g + 8] for g in range(4)], axis=1)
    copies = [pltpu.make_async_copy(out_ref, out_hbm.at[n], out_sem.at[n]) for n in range(16)]
    for copy in copies:
        copy.start()
    for copy in copies:
        copy.wait()


def tree_kernel(
    where_ref, got_ref, shift_ref, signs_ref, send_ref, held_ref, level_ref, span_ref
):
    me = where_ref[0]
    group = where_ref[1]
    lane = lax.broadcasted_iota(jnp.int32, (128, 128), 1)
    tails = got_ref[:, 64:72, :].reshape(128, 128)
    turned = tails.T
    dest_row = jnp.concatenate([turned[32 * g + 30 : 32 * g + 31] for g in range(4)], axis=1)
    spot = lax.broadcasted_iota(jnp.int32, (1, GROUP), 1)
    block_row = ((spot // 8) % 16) * 32 + (spot // 128) * 8 + spot % 8
    key_row = dest_row * 512.0 + block_row.astype(F32)
    spot = lax.broadcasted_iota(jnp.int32, (128, 1), 0)
    high_parts, low_parts, pair_parts, key_parts = [], [], [], []
    for g in range(4):
        tail = tails if g == 0 else pltpu.roll(tails, 128 - 32 * g, 1)
        block = (spot // 8) * 32 + g * 8 + spot % 8
        key_parts.append(tail[:, 30:31] * 512.0 + block.astype(F32))
        first = got_ref[:, 8 * g : 8 * g + 8, :].reshape(128, 128)
        second = got_ref[:, 32 + 8 * g : 40 + 8 * g, :].reshape(128, 128)
        tail = jnp.where(lane < 30, tail, 0.0)
        top = tail.astype(BF16).astype(F32)
        pair = top + pltpu.roll(tail - top, 32, 1)
        (first_high, first_low), (second_high, second_low) = split(first), split(second)
        high_parts.append(jnp.concatenate([first_high, second_high], axis=1))
        low_parts.append(jnp.concatenate([first_low, second_low], axis=1))
        pair_parts.append(pair.astype(BF16))
    held = jnp.concatenate(
        [
            jnp.concatenate(high_parts, axis=0),
            jnp.concatenate(low_parts, axis=0),
            jnp.concatenate(pair_parts, axis=0),
        ],
        axis=1,
    )
    smaller = jnp.zeros((8, GROUP), F32)
    for g in range(4):
        less = jnp.where(key_parts[g] < key_row, 1.0, 0.0)
        smaller = smaller + jnp.sum(less.reshape(16, 8, GROUP), axis=0)
    rank = jnp.sum(smaller, axis=0, keepdims=True).astype(jnp.int32)
    mine = me.astype(F32)
    start = jnp.sum(jnp.where(dest_row < mine, 1.0, 0.0), axis=1, keepdims=True).astype(jnp.int32)
    tally = jnp.sum(jnp.where(dest_row == mine, 1.0, 0.0), axis=1, keepdims=True).astype(jnp.int32)
    row = lax.broadcasted_iota(jnp.int32, (GROUP, 1), 0)
    turned_row = (row % 8) * 64 + ((row // 8) % 8) * 8 + row // 64
    slot = lax.broadcasted_iota(jnp.int32, (128, 1), 0)
    wanted = jnp.concatenate([turned_row, jnp.where(slot < tally, start + slot, -1)], axis=0)
    chosen = jnp.where(wanted == rank, 1.0, 0.0).astype(BF16)
    placed = jnp.dot(chosen, held, preferred_element_type=F32)
    own = placed[GROUP:]
    own_tail = own[:, 512:640]
    held_ref[:, 0:256] = own[:, 0:256] + own[:, 256:512]
    held_ref[:, 256:384] = own_tail + pltpu.roll(own_tail, 96, 1)
    shift = shift_ref[...]
    tiny = 2.0**-P_SIZE

    def moved(high, low):
        stacked = jnp.dot(
            jnp.concatenate([high, low], axis=0), shift, preferred_element_type=F32
        )
        count = high.shape[0]
        return stacked[:count] + stacked[count:]

    def signed(octant):
        return signs_ref[octant : octant + 1, :]

    sign_rows = jnp.concatenate(
        [jnp.broadcast_to(signed(o)[:, 0:256], (64, 256)) for o in range(8)], axis=0
    )
    sons = placed[:GROUP]
    high = (sons[:, 0:256] * sign_rows).astype(BF16)
    low = (sons[:, 256:512] * sign_rows).astype(BF16)
    parts = moved(high, low)
    level = parts[0:64] * signed(0)
    tail_sum = sons[0:64, 512:640]
    for o in range(1, 8):
        level = level + parts[64 * o : 64 * o + 64] * signed(o)
        tail_sum = tail_sum + sons[64 * o : 64 * o + 64, 512:640]
    tail_lane = lax.broadcasted_iota(jnp.int32, (1, 128), 1) < 30

    def with_tail(body, tail):
        added = body[:, 256:384] + jnp.where(tail_lane, tail * tiny, 0.0)
        return jnp.concatenate([body[:, 0:256], added], axis=1)

    level_1 = with_tail(level, tail_sum + pltpu.roll(tail_sum, 96, 1))
    sign_rows = jnp.concatenate(
        [jnp.broadcast_to(signed(o), (8, 384)) for o in range(8)], axis=0
    )
    parts = moved(*split(level_1[:, 0:256] * sign_rows[:, 0:256])) * sign_rows
    level = jnp.sum(parts.reshape(8, 8, 384), axis=0)
    tail_sum = jnp.sum(level_1[:, 256:384].reshape(8, 8, 128), axis=0)
    level_2 = with_tail(level, tail_sum)
    all_signs = signs_ref[...]
    parts = moved(*split(level_2[:, 0:256] * all_signs[:, 0:256])) * all_signs
    level = jnp.sum(parts, axis=0, keepdims=True)
    tail_sum = jnp.sum(level_2[:, 256:384], axis=0, keepdims=True)
    level_3 = with_tail(level, tail_sum)
    sublane = lax.broadcasted_iota(jnp.int32, (8, 384), 0)

    def share(value, octant):
        sign = jnp.sum(jnp.where(sublane == octant, all_signs, 0.0), axis=0, keepdims=True)
        eight = jnp.broadcast_to(value * sign, (8, 384))
        part = moved(*split(eight[:, 0:256]))[0:1] * sign
        return with_tail(part, value[:, 256:384])

    level_4 = share(level_3, group % 8)
    level_5 = share(level_4, group // 8)
    send_ref[0:1] = level_4
    send_ref[1:2] = level_5
    level_ref[0:64] = level_1
    level_ref[64:72] = level_2
    level_ref[72:80] = jnp.broadcast_to(level_3, (8, 384))
    span_ref[0:1] = jnp.broadcast_to(start, (1, 128))
    span_ref[1:2] = jnp.broadcast_to(start + tally, (1, 128))
    span_ref[2:3] = jnp.zeros((1, 128), jnp.int32) + jnp.where(group % 8 == 0, 22, -1)
    span_ref[3:4] = jnp.zeros((1, 128), jnp.int32) + jnp.where(group == 0, 24, -1)


def outputs_kernel(held_ref, level_ref, span_ref, leaf_ref, box_ref):
    held = held_ref[...]
    leaf_ref[0:128] = held[:, 0:128].T
    leaf_ref[128:256] = held[:, 128:256].T
    leaf_ref[256:COEFS] = held[:, 256:384].T[0 : COEFS - 256]
    start = span_ref[0:1, 0:1]
    end = span_ref[1:2, 0:1]
    out_slot = lax.broadcasted_iota(jnp.int32, (32, 1), 0)
    box_1 = start // 8 + out_slot
    box_2 = start // 64 + out_slot - 17
    source = jnp.where((box_1 * 8 >= start) & (box_1 * 8 < end), (box_1 % 8) * 8 + box_1 // 8, -1)
    source_2 = jnp.where((box_2 * 64 >= start) & (box_2 * 64 < end), 64 + box_2, -1)
    first_of_group = (start == 0) & (end > 0)
    source_3 = jnp.where(first_of_group & (out_slot == 20), 72, -1)
    source = jnp.where(out_slot < 17, source, jnp.where(out_slot < 20, source_2, source_3))
    column = lax.broadcasted_iota(jnp.int32, (32, 128), 1)
    select = jnp.where(column == source, 1.0, 0.0).astype(BF16)
    boxes = jnp.concatenate([level_ref[...], jnp.zeros((48, 384), F32)], axis=0)
    high, low = split(boxes)
    picked = jnp.dot(select, high, preferred_element_type=F32) + jnp.dot(
        select, low, preferred_element_type=F32
    )
    upper = (out_slot == span_ref[2:3, 0:1]) | (out_slot == span_ref[3:4, 0:1])
    owned = first_of_group & upper
    picked = picked + jnp.where(owned, 1.0, 0.0)
    box_ref[...] = picked[0:26, 0:COEFS]


def permute(value, *pairs):
    return lax.ppermute(value, "wide", list(pairs))


def across(share, kept):
    four = permute(share, *((8 + i, i) for i in range(4)))
    pair = share + permute(share, *((2 * i + 1, 2 * i) for i in range(16)))
    eight = permute(pair, (16, 0), (18, 1))
    ten = permute(pair, (20, 0), (22, 1))
    twelve = permute(pair, (24, 0), (26, 1))
    six = permute(pair, (12, 0), (14, 1))
    after, four, kept = lax.optimization_barrier((pair, four, kept))
    fourteen = permute(after, (28, 0), (30, 1))
    row = lax.broadcasted_iota(jnp.int32, (2, 384), 0)
    mixed = share + jnp.where(row == 0, 0.0, four)
    quads = [[8 * q + j for j in range(8)] for q in range(4)]
    spread = jnp.broadcast_to(mixed[None], (8, 2, 384))
    quad = jnp.sum(
        lax.all_to_all(spread, "wide", 0, 0, axis_index_groups=quads, tiled=True), axis=0
    )
    leaf, box = outputs(*kept)
    late = eight + ten + twelve + six + fourteen
    late, box = lax.optimization_barrier((late, box))
    return quad, quad + late + permute(late, (1, 0)), leaf, box


VMEM = pl.BlockSpec(memory_space=pltpu.VMEM)
HBM = pl.BlockSpec(memory_space=pltpu.HBM)
SMEM = pl.BlockSpec(memory_space=pltpu.SMEM)
PARAMS = pltpu.CompilerParams(vmem_limit_bytes=40 * 1024 * 1024)


def outputs(held, levels, span):
    return pl.pallas_call(
        outputs_kernel,
        out_shape=(
            jax.ShapeDtypeStruct((COEFS, 128), F32),
            jax.ShapeDtypeStruct((26, COEFS), F32),
        ),
        in_specs=[VMEM] * 3,
        out_specs=(VMEM,) * 2,
        compiler_params=PARAMS,
    )(held, levels, span)


def shards(positions, moments, counts, dest):
    shift, signs = tables()
    where = jnp.stack([lax.axis_index("narrow"), lax.axis_index("wide")]).astype(jnp.int32)
    sent = pl.pallas_call(
        moments_kernel,
        out_shape=jax.ShapeDtypeStruct((16, 72, 128), F32),
        in_specs=[HBM] * 4,
        out_specs=HBM,
        scratch_shapes=[
            pltpu.VMEM((3, 32, 256), F32),
            pltpu.VMEM((3, 32, 256), F32),
            pltpu.VMEM((1, 32), jnp.int32),
            pltpu.VMEM((1, 32), jnp.int32),
            pltpu.VMEM((72, 128), F32),
            pltpu.VMEM((6, 64, 128), F32),
            pltpu.VMEM((288, 8, 128), F32),
            pltpu.SemaphoreType.DMA((8,)),
            pltpu.SemaphoreType.DMA((16,)),
        ],
        compiler_params=pltpu.CompilerParams(vmem_limit_bytes=64 * 1024 * 1024 - 65536),
    )(
        jnp.transpose(positions, (1, 0, 2)),
        jnp.transpose(moments, (1, 0, 2)),
        counts.reshape(1, 32),
        dest.reshape(1, 32),
    )
    got = lax.all_to_all(sent, "narrow", split_axis=0, concat_axis=0, tiled=True)
    share, *kept = pl.pallas_call(
        tree_kernel,
        out_shape=(
            jax.ShapeDtypeStruct((2, 384), F32),
            jax.ShapeDtypeStruct((128, 384), F32),
            jax.ShapeDtypeStruct((80, 384), F32),
            jax.ShapeDtypeStruct((4, 128), jnp.int32),
        ),
        in_specs=[SMEM, VMEM, VMEM, VMEM],
        out_specs=(VMEM,) * 4,
        compiler_params=PARAMS,
    )(where, got, jnp.asarray(shift, BF16), jnp.asarray(signs, F32))
    quad, top, leaf, box = across(share, kept)
    row = lax.broadcasted_iota(jnp.int32, (26, COEFS), 0)
    last = jnp.where(row == 24, top[1:2, 0:COEFS], 1.0)
    box = box * jnp.where(row == 22, quad[0:1, 0:COEFS], last)
    return leaf.T, box


def solution(mesh):
    both = ("wide", "narrow")
    placed = (P(both, None, None), P(both, None, None), P(both), P(both))
    return jax.shard_map(
        shards,
        mesh=mesh,
        in_specs=placed,
        out_specs=(P(both, None), P(both, None)),
        check_vma=False,
    )
```

```python
import math

import jax
import jax.numpy as jnp
import numpy as np
from jax import lax
from jax.experimental import pallas as pl
from jax.experimental.pallas import tpu as pltpu
from jax.sharding import PartitionSpec as P

P_SIZE = 10
COEFS = 286
GROUP = 512
F32 = jnp.float32
BF16 = jnp.bfloat16


def exponent_list(order):
    triples = []
    for degree in range(order + 1):
        for power_x in range(degree, -1, -1):
            for power_y in range(degree - power_x, -1, -1):
                triples.append((power_x, power_y, degree - power_x - power_y))
    return triples


def tables():
    triples = exponent_list(P_SIZE)
    shift = np.zeros((256, 384), np.float32)
    for column, target in enumerate(triples):
        for row, source in enumerate(triples[:256]):
            if all(s <= t for s, t in zip(source, target)):
                shift[row, column] = 0.5 ** sum(target) * math.prod(
                    math.comb(t, s) for s, t in zip(source, target)
                )
    signs = np.ones((8, 384), np.float32)
    for octant in range(8):
        for column, target in enumerate(triples):
            for axis in range(3):
                if not (octant >> axis) & 1 and target[axis] % 2:
                    signs[octant, column] = -signs[octant, column]
    return shift, signs


def split(value):
    high = value.astype(BF16)
    return high, (value - high.astype(F32)).astype(BF16)


def moments_kernel(
    places_hbm, dipoles_hbm, counts_hbm, dest_hbm, out_hbm,
    places_ref, dipoles_ref, counts_ref, dest_ref, out_ref, grid_ref, sums_ref, in_sems, out_sem,
):
    pairs = [(counts_hbm, counts_ref), (dest_hbm, dest_ref)]
    for axis in range(3):
        pairs.append((places_hbm.at[axis], places_ref.at[axis]))
        pairs.append((dipoles_hbm.at[axis], dipoles_ref.at[axis]))
    copies = [pltpu.make_async_copy(a, b, in_sems.at[k]) for k, (a, b) in enumerate(pairs)]
    for copy in copies:
        copy.start()
    sums_ref[...] = jnp.zeros(sums_ref.shape, F32)
    for copy in copies:
        copy.wait()
    index_of = {triple: i for i, triple in enumerate(exponent_list(P_SIZE))}

    def turned(values):
        quarters = [values[:, 64 * q : 64 * q + 64] for q in range(4)]
        return jnp.concatenate(quarters, axis=0).T

    live = jnp.concatenate([counts_ref[...]] * 4, axis=1)
    rows = lax.broadcasted_iota(jnp.int32, (64, 128), 0)
    lanes = lax.broadcasted_iota(jnp.int32, (64, 128), 1)
    living = rows + 64 * (lanes // 32) < live
    for axis in range(3):
        grid_ref[axis] = turned(places_ref[axis])
        grid_ref[3 + axis] = jnp.where(living, turned(dipoles_ref[axis]), 0.0)

    def stripe(step, carry):
        picked = pl.ds(pl.multiple_of(step * 32, 32), 32)
        x, y, z, mx, my, mz = [grid_ref[k, picked, :] for k in range(6)]

        def note(triple, psi):
            folded = (psi[0:8] + psi[8:16]) + (psi[16:24] + psi[24:32])
            sums_ref[index_of[triple]] += folded

        phi_x, psi_x = None, None
        for a in range(P_SIZE + 1):
            if a == 1:
                phi_x, psi_x = x, mx
            elif a > 1:
                phi_x, psi_x = phi_x * x, psi_x * x + mx * phi_x
            phi, psi = phi_x, psi_x
            for e in range(P_SIZE + 1 - a):
                if e > 0:
                    if phi is None:
                        phi, psi = y, my
                    else:
                        phi, psi = phi * y, psi * y + my * phi
                if psi is not None:
                    note((a, e, 0), psi)
                deep, omega = psi, mz if phi is None else mz * phi
                for c in range(1, P_SIZE + 1 - a - e):
                    deep = omega if deep is None else deep * z + omega
                    note((a, e, c), deep)
                    omega = omega * z
        return carry

    lax.fori_loop(0, 2, stripe, 0)
    folded = jnp.sum(sums_ref[...], axis=1)
    blank = jnp.zeros((1, 96), F32)
    where_to = jnp.concatenate([dest_ref[...].astype(F32), blank], axis=1)
    row = lax.broadcasted_iota(jnp.int32, folded.shape, 0)
    folded = jnp.where(row == COEFS, where_to, folded * (1.0 / 16.0))
    folded = jnp.concatenate([folded, jnp.zeros((96, 128), F32)], axis=0).T
    values = (folded[0:32] + folded[32:64]) + (folded[64:96] + folded[96:128])
    out_ref[0:32] = values[:, 0:128]
    out_ref[32:64] = values[:, 128:256]
    tail = values[:, 256:288]
    out_ref[64:72] = jnp.concatenate([tail[8 * g : 8 * g + 8] for g in range(4)], axis=1)
    copies = [pltpu.make_async_copy(out_ref, out_hbm.at[n], out_sem.at[n]) for n in range(16)]
    for copy in copies:
        copy.start()
    for copy in copies:
        copy.wait()


def group_values(got_ref):
    lane = lax.broadcasted_iota(jnp.int32, (128, 128), 1)
    tails = got_ref[:, 64:72, :].reshape(128, 128)
    high_parts, low_parts, pair_parts = [], [], []
    for g in range(4):
        tail = tails if g == 0 else pltpu.roll(tails, 128 - 32 * g, 1)
        first = got_ref[:, 8 * g : 8 * g + 8, :].reshape(128, 128)
        second = got_ref[:, 32 + 8 * g : 40 + 8 * g, :].reshape(128, 128)
        tail = jnp.where(lane < 30, tail, 0.0)
        top = tail.astype(BF16).astype(F32)
        pair = top + pltpu.roll(tail - top, 32, 1)
        (first_high, first_low), (second_high, second_low) = split(first), split(second)
        high_parts.append(jnp.concatenate([first_high, second_high], axis=1))
        low_parts.append(jnp.concatenate([first_low, second_low], axis=1))
        pair_parts.append(pair.astype(BF16))
    parts = [jnp.concatenate(p, axis=0) for p in (high_parts, low_parts, pair_parts)]
    return jnp.concatenate(parts, axis=1)


def tree_kernel(
    where_ref, got_ref, shift_ref, signs_ref, send_ref, rank_ref, level_ref, span_ref
):
    me = where_ref[0]
    group = where_ref[1]
    tails = got_ref[:, 64:72, :].reshape(128, 128)
    turned = tails.T
    dest_row = jnp.concatenate([turned[32 * g + 30 : 32 * g + 31] for g in range(4)], axis=1)
    spot = lax.broadcasted_iota(jnp.int32, (1, GROUP), 1)
    block_row = ((spot // 8) % 16) * 32 + (spot // 128) * 8 + spot % 8
    key_row = dest_row * 512.0 + block_row.astype(F32)
    spot = lax.broadcasted_iota(jnp.int32, (128, 1), 0)
    key_parts = []
    for g in range(4):
        block = (spot // 8) * 32 + g * 8 + spot % 8
        key_parts.append(tails[:, 32 * g + 30 : 32 * g + 31] * 512.0 + block.astype(F32))
    held = group_values(got_ref)
    smaller = jnp.zeros((8, GROUP), F32)
    for g in range(4):
        less = jnp.where(key_parts[g] < key_row, 1.0, 0.0)
        smaller = smaller + jnp.sum(less.reshape(16, 8, GROUP), axis=0)
    rank = jnp.sum(smaller, axis=0, keepdims=True).astype(jnp.int32)
    mine = me.astype(F32)
    start = jnp.sum(jnp.where(dest_row < mine, 1.0, 0.0), axis=1, keepdims=True).astype(jnp.int32)
    tally = jnp.sum(jnp.where(dest_row == mine, 1.0, 0.0), axis=1, keepdims=True).astype(jnp.int32)
    row = lax.broadcasted_iota(jnp.int32, (GROUP, 1), 0)
    turned_row = (row % 8) * 64 + ((row // 8) % 8) * 8 + row // 64
    chosen = jnp.where(turned_row == rank, 1.0, 0.0).astype(BF16)
    sons = jnp.dot(chosen, held, preferred_element_type=F32)
    rank_ref[...] = rank
    shift = shift_ref[...]
    tiny = 2.0**-P_SIZE

    def moved(high, low):
        stacked = jnp.dot(
            jnp.concatenate([high, low], axis=0), shift, preferred_element_type=F32
        )
        count = high.shape[0]
        return stacked[:count] + stacked[count:]

    def signed(octant):
        return signs_ref[octant : octant + 1, :]

    sign_rows = jnp.concatenate(
        [jnp.broadcast_to(signed(o)[:, 0:256], (64, 256)) for o in range(8)], axis=0
    )
    high = (sons[:, 0:256] * sign_rows).astype(BF16)
    low = (sons[:, 256:512] * sign_rows).astype(BF16)
    parts = moved(high, low)
    level = parts[0:64] * signed(0)
    tail_sum = sons[0:64, 512:640]
    for o in range(1, 8):
        level = level + parts[64 * o : 64 * o + 64] * signed(o)
        tail_sum = tail_sum + sons[64 * o : 64 * o + 64, 512:640]
    tail_lane = lax.broadcasted_iota(jnp.int32, (1, 128), 1) < 30

    def with_tail(body, tail):
        added = body[:, 256:384] + jnp.where(tail_lane, tail * tiny, 0.0)
        return jnp.concatenate([body[:, 0:256], added], axis=1)

    level_1 = with_tail(level, tail_sum + pltpu.roll(tail_sum, 96, 1))
    sign_rows = jnp.concatenate(
        [jnp.broadcast_to(signed(o), (8, 384)) for o in range(8)], axis=0
    )
    parts = moved(*split(level_1[:, 0:256] * sign_rows[:, 0:256])) * sign_rows
    level = jnp.sum(parts.reshape(8, 8, 384), axis=0)
    tail_sum = jnp.sum(level_1[:, 256:384].reshape(8, 8, 128), axis=0)
    level_2 = with_tail(level, tail_sum)
    all_signs = signs_ref[...]
    parts = moved(*split(level_2[:, 0:256] * all_signs[:, 0:256])) * all_signs
    level = jnp.sum(parts, axis=0, keepdims=True)
    tail_sum = jnp.sum(level_2[:, 256:384], axis=0, keepdims=True)
    level_3 = with_tail(level, tail_sum)
    sublane = lax.broadcasted_iota(jnp.int32, (8, 384), 0)

    def share(value, octant):
        sign = jnp.sum(jnp.where(sublane == octant, all_signs, 0.0), axis=0, keepdims=True)
        eight = jnp.broadcast_to(value * sign, (8, 384))
        part = moved(*split(eight[:, 0:256]))[0:1] * sign
        return with_tail(part, value[:, 256:384])

    level_4 = share(level_3, group % 8)
    level_5 = share(level_4, group // 8)
    send_ref[0:1] = level_4
    send_ref[1:2] = level_5
    level_ref[0:64] = level_1
    level_ref[64:72] = level_2
    level_ref[72:80] = jnp.broadcast_to(level_3, (8, 384))
    span_ref[0:1] = jnp.broadcast_to(start, (1, 128))
    span_ref[1:2] = jnp.broadcast_to(start + tally, (1, 128))
    span_ref[2:3] = jnp.zeros((1, 128), jnp.int32) + jnp.where(group % 8 == 0, 22, -1)
    span_ref[3:4] = jnp.zeros((1, 128), jnp.int32) + jnp.where(group == 0, 24, -1)


def outputs_kernel(got_ref, rank_ref, level_ref, span_ref, leaf_ref, box_ref):
    start = span_ref[0:1, 0:1]
    end = span_ref[1:2, 0:1]
    slot = start + lax.broadcasted_iota(jnp.int32, (128, 1), 0)
    chosen = jnp.where(jnp.where(slot < end, slot, -1) == rank_ref[...], 1.0, 0.0).astype(BF16)
    own = jnp.dot(chosen, group_values(got_ref), preferred_element_type=F32)
    own_tail = own[:, 512:640]
    leaf_ref[0:128] = (own[:, 0:128] + own[:, 256:384]).T
    leaf_ref[128:256] = (own[:, 128:256] + own[:, 384:512]).T
    leaf_ref[256:COEFS] = (own_tail + pltpu.roll(own_tail, 96, 1)).T[0 : COEFS - 256]
    out_slot = lax.broadcasted_iota(jnp.int32, (32, 1), 0)
    box_1 = start // 8 + out_slot
    box_2 = start // 64 + out_slot - 17
    source = jnp.where((box_1 * 8 >= start) & (box_1 * 8 < end), (box_1 % 8) * 8 + box_1 // 8, -1)
    source_2 = jnp.where((box_2 * 64 >= start) & (box_2 * 64 < end), 64 + box_2, -1)
    first_of_group = (start == 0) & (end > 0)
    source_3 = jnp.where(first_of_group & (out_slot == 20), 72, -1)
    source = jnp.where(out_slot < 17, source, jnp.where(out_slot < 20, source_2, source_3))
    column = lax.broadcasted_iota(jnp.int32, (32, 128), 1)
    select = jnp.where(column == source, 1.0, 0.0).astype(BF16)
    boxes = jnp.concatenate([level_ref[...], jnp.zeros((48, 384), F32)], axis=0)
    high, low = split(boxes)
    picked = jnp.dot(select, high, preferred_element_type=F32) + jnp.dot(
        select, low, preferred_element_type=F32
    )
    upper = (out_slot == span_ref[2:3, 0:1]) | (out_slot == span_ref[3:4, 0:1])
    owned = first_of_group & upper
    picked = picked + jnp.where(owned, 1.0, 0.0)
    box_ref[...] = picked[0:26, 0:COEFS]


def permute(value, *pairs):
    return lax.ppermute(value, "wide", list(pairs))


def across(share, got, kept):
    four = permute(share, *((8 + i, i) for i in range(6)))
    pair = share + permute(share, *((2 * i + 1, 2 * i) for i in range(16)))
    eight = permute(pair, (16, 0))
    nine = permute(pair, (18, 1), (20, 0))
    seven = permute(pair, (14, 0), (22, 1))
    twelve = permute(pair, (24, 0), (26, 1))
    after, four, kept = lax.optimization_barrier((pair, four, kept))
    fourteen = permute(after, (28, 0), (30, 1))
    quads = [[8 * q + j for j in range(8)] for q in range(4)]
    row = lax.broadcasted_iota(jnp.int32, (8, 2, 384), 1)
    spread = share[None] + jnp.where(row == 0, 0.0, four[None])
    quad = jnp.sum(
        lax.all_to_all(spread, "wide", 0, 0, axis_index_groups=quads, tiled=True), axis=0
    )
    leaf, box = outputs(got, *kept)
    late = twelve + seven + nine + fourteen
    late, box = lax.optimization_barrier((late, box))
    return quad, quad + late + eight + permute(late, (1, 0)), leaf, box


VMEM = pl.BlockSpec(memory_space=pltpu.VMEM)
HBM = pl.BlockSpec(memory_space=pltpu.HBM)
SMEM = pl.BlockSpec(memory_space=pltpu.SMEM)
PARAMS = pltpu.CompilerParams(vmem_limit_bytes=40 * 1024 * 1024)


def outputs(got, rank, levels, span):
    return pl.pallas_call(
        outputs_kernel,
        out_shape=(
            jax.ShapeDtypeStruct((COEFS, 128), F32),
            jax.ShapeDtypeStruct((26, COEFS), F32),
        ),
        in_specs=[VMEM] * 4,
        out_specs=(VMEM,) * 2,
        compiler_params=PARAMS,
    )(got, rank, levels, span)


def shards(positions, moments, counts, dest):
    shift, signs = tables()
    where = jnp.stack([lax.axis_index("narrow"), lax.axis_index("wide")]).astype(jnp.int32)
    sent = pl.pallas_call(
        moments_kernel,
        out_shape=jax.ShapeDtypeStruct((16, 72, 128), F32),
        in_specs=[HBM] * 4,
        out_specs=HBM,
        scratch_shapes=[
            pltpu.VMEM((3, 32, 256), F32),
            pltpu.VMEM((3, 32, 256), F32),
            pltpu.VMEM((1, 32), jnp.int32),
            pltpu.VMEM((1, 32), jnp.int32),
            pltpu.VMEM((72, 128), F32),
            pltpu.VMEM((6, 64, 128), F32),
            pltpu.VMEM((288, 8, 128), F32),
            pltpu.SemaphoreType.DMA((8,)),
            pltpu.SemaphoreType.DMA((16,)),
        ],
        compiler_params=pltpu.CompilerParams(vmem_limit_bytes=64 * 1024 * 1024 - 65536),
    )(
        jnp.transpose(positions, (1, 0, 2)),
        jnp.transpose(moments, (1, 0, 2)),
        counts.reshape(1, 32),
        dest.reshape(1, 32),
    )
    got = lax.all_to_all(sent, "narrow", split_axis=0, concat_axis=0, tiled=True)
    share, *kept = pl.pallas_call(
        tree_kernel,
        out_shape=(
            jax.ShapeDtypeStruct((2, 384), F32),
            jax.ShapeDtypeStruct((1, GROUP), jnp.int32),
            jax.ShapeDtypeStruct((80, 384), F32),
            jax.ShapeDtypeStruct((4, 128), jnp.int32),
        ),
        in_specs=[SMEM, VMEM, VMEM, VMEM],
        out_specs=(VMEM,) * 4,
        compiler_params=PARAMS,
    )(where, got, jnp.asarray(shift, BF16), jnp.asarray(signs, F32))
    quad, top, leaf, box = across(share, got, kept)
    row = lax.broadcasted_iota(jnp.int32, (26, COEFS), 0)
    last = jnp.where(row == 24, top[1:2, 0:COEFS], 1.0)
    box = box * jnp.where(row == 22, quad[0:1, 0:COEFS], last)
    return leaf.T, box


def solution(mesh):
    both = ("wide", "narrow")
    placed = (P(both, None, None), P(both, None, None), P(both), P(both))
    return jax.shard_map(
        shards,
        mesh=mesh,
        in_specs=placed,
        out_specs=(P(both, None), P(both, None)),
        check_vma=False,
    )
```

```python
import math

import jax
import jax.numpy as jnp
import numpy as np
from jax import lax
from jax.experimental import pallas as pl
from jax.experimental.pallas import tpu as pltpu
from jax.sharding import PartitionSpec as P

P_SIZE = 10
COEFS = 286
GROUP = 512
F32 = jnp.float32
BF16 = jnp.bfloat16


def exponent_list(order):
    triples = []
    for degree in range(order + 1):
        for power_x in range(degree, -1, -1):
            for power_y in range(degree - power_x, -1, -1):
                triples.append((power_x, power_y, degree - power_x - power_y))
    return triples


def tables():
    triples = exponent_list(P_SIZE)
    shift = np.zeros((256, 384), np.float32)
    for column, target in enumerate(triples):
        for row, source in enumerate(triples[:256]):
            if all(s <= t for s, t in zip(source, target)):
                shift[row, column] = 0.5 ** sum(target) * math.prod(
                    math.comb(t, s) for s, t in zip(source, target)
                )
    signs = np.ones((8, 384), np.float32)
    for octant in range(8):
        for column, target in enumerate(triples):
            for axis in range(3):
                if not (octant >> axis) & 1 and target[axis] % 2:
                    signs[octant, column] = -signs[octant, column]
    return shift, signs


def split(value):
    high = value.astype(BF16)
    return high, (value - high.astype(F32)).astype(BF16)


def moments_kernel(
    places_hbm, dipoles_hbm, counts_hbm, dest_hbm, out_hbm,
    places_ref, dipoles_ref, counts_ref, dest_ref, out_ref, grid_ref, sums_ref, in_sems, out_sem,
):
    pairs = [(counts_hbm, counts_ref), (dest_hbm, dest_ref)]
    for axis in range(3):
        pairs.append((places_hbm.at[axis], places_ref.at[axis]))
        pairs.append((dipoles_hbm.at[axis], dipoles_ref.at[axis]))
    copies = [pltpu.make_async_copy(a, b, in_sems.at[k]) for k, (a, b) in enumerate(pairs)]
    for copy in copies:
        copy.start()
    sums_ref[...] = jnp.zeros(sums_ref.shape, F32)
    for copy in copies:
        copy.wait()
    index_of = {triple: i for i, triple in enumerate(exponent_list(P_SIZE))}

    def turned(values):
        quarters = [values[:, 64 * q : 64 * q + 64] for q in range(4)]
        return jnp.concatenate(quarters, axis=0).T

    live = jnp.concatenate([counts_ref[...]] * 4, axis=1)
    rows = lax.broadcasted_iota(jnp.int32, (64, 128), 0)
    lanes = lax.broadcasted_iota(jnp.int32, (64, 128), 1)
    living = rows + 64 * (lanes // 32) < live
    for axis in range(3):
        grid_ref[axis] = turned(places_ref[axis])
        grid_ref[3 + axis] = jnp.where(living, turned(dipoles_ref[axis]), 0.0)

    def stripe(step, carry):
        picked = pl.ds(pl.multiple_of(step * 32, 32), 32)
        x, y, z, mx, my, mz = [grid_ref[k, picked, :] for k in range(6)]

        def note(triple, psi):
            folded = (psi[0:8] + psi[8:16]) + (psi[16:24] + psi[24:32])
            sums_ref[index_of[triple]] += folded

        phi_x, psi_x = None, None
        for a in range(P_SIZE + 1):
            if a == 1:
                phi_x, psi_x = x, mx
            elif a > 1:
                phi_x, psi_x = phi_x * x, psi_x * x + mx * phi_x
            phi, psi = phi_x, psi_x
            for e in range(P_SIZE + 1 - a):
                if e > 0:
                    if phi is None:
                        phi, psi = y, my
                    else:
                        phi, psi = phi * y, psi * y + my * phi
                if psi is not None:
                    note((a, e, 0), psi)
                deep, omega = psi, mz if phi is None else mz * phi
                for c in range(1, P_SIZE + 1 - a - e):
                    deep = omega if deep is None else deep * z + omega
                    note((a, e, c), deep)
                    omega = omega * z
        return carry

    lax.fori_loop(0, 2, stripe, 0)
    folded = jnp.sum(sums_ref[...], axis=1)
    blank = jnp.zeros((1, 96), F32)
    where_to = jnp.concatenate([dest_ref[...].astype(F32), blank], axis=1)
    row = lax.broadcasted_iota(jnp.int32, folded.shape, 0)
    folded = jnp.where(row == COEFS, where_to, folded * (1.0 / 16.0))
    folded = jnp.concatenate([folded, jnp.zeros((96, 128), F32)], axis=0).T
    values = (folded[0:32] + folded[32:64]) + (folded[64:96] + folded[96:128])
    out_ref[0:32] = values[:, 0:128]
    out_ref[32:64] = values[:, 128:256]
    tail = values[:, 256:288]
    out_ref[64:72] = jnp.concatenate([tail[8 * g : 8 * g + 8] for g in range(4)], axis=1)
    copies = [pltpu.make_async_copy(out_ref, out_hbm.at[n], out_sem.at[n]) for n in range(16)]
    for copy in copies:
        copy.start()
    for copy in copies:
        copy.wait()


def group_values(got_ref):
    lane = lax.broadcasted_iota(jnp.int32, (128, 128), 1)
    tails = got_ref[:, 64:72, :].reshape(128, 128)
    high_parts, low_parts, pair_parts = [], [], []
    for g in range(4):
        tail = tails if g == 0 else pltpu.roll(tails, 128 - 32 * g, 1)
        first = got_ref[:, 8 * g : 8 * g + 8, :].reshape(128, 128)
        second = got_ref[:, 32 + 8 * g : 40 + 8 * g, :].reshape(128, 128)
        tail = jnp.where(lane < 30, tail, 0.0)
        top = tail.astype(BF16).astype(F32)
        pair = top + pltpu.roll(tail - top, 32, 1)
        (first_high, first_low), (second_high, second_low) = split(first), split(second)
        high_parts.append(jnp.concatenate([first_high, second_high], axis=1))
        low_parts.append(jnp.concatenate([first_low, second_low], axis=1))
        pair_parts.append(pair.astype(BF16))
    parts = [jnp.concatenate(p, axis=0) for p in (high_parts, low_parts, pair_parts)]
    return jnp.concatenate(parts, axis=1)


def tree_kernel(
    where_ref, got_ref, shift_ref, signs_ref, send_ref, rank_ref, level_ref, span_ref
):
    me = where_ref[0]
    group = where_ref[1]
    tails = got_ref[:, 64:72, :].reshape(128, 128)
    turned = tails.T
    dest_row = jnp.concatenate([turned[32 * g + 30 : 32 * g + 31] for g in range(4)], axis=1)
    spot = lax.broadcasted_iota(jnp.int32, (1, GROUP), 1)
    block_row = ((spot // 8) % 16) * 32 + (spot // 128) * 8 + spot % 8
    key_row = dest_row * 512.0 + block_row.astype(F32)
    spot = lax.broadcasted_iota(jnp.int32, (128, 1), 0)
    key_parts = []
    for g in range(4):
        block = (spot // 8) * 32 + g * 8 + spot % 8
        key_parts.append(tails[:, 32 * g + 30 : 32 * g + 31] * 512.0 + block.astype(F32))
    held = group_values(got_ref)
    smaller = jnp.zeros((8, GROUP), F32)
    for g in range(4):
        less = jnp.where(key_parts[g] < key_row, 1.0, 0.0)
        smaller = smaller + jnp.sum(less.reshape(16, 8, GROUP), axis=0)
    rank = jnp.sum(smaller, axis=0, keepdims=True).astype(jnp.int32)
    mine = me.astype(F32)
    start = jnp.sum(jnp.where(dest_row < mine, 1.0, 0.0), axis=1, keepdims=True).astype(jnp.int32)
    tally = jnp.sum(jnp.where(dest_row == mine, 1.0, 0.0), axis=1, keepdims=True).astype(jnp.int32)
    row = lax.broadcasted_iota(jnp.int32, (GROUP, 1), 0)
    turned_row = (row % 8) * 64 + ((row // 8) % 8) * 8 + row // 64
    chosen = jnp.where(turned_row == rank, 1.0, 0.0).astype(BF16)
    sons = jnp.dot(chosen, held, preferred_element_type=F32)
    rank_ref[...] = rank
    shift = shift_ref[...]
    tiny = 2.0**-P_SIZE

    def moved(high, low):
        stacked = jnp.dot(
            jnp.concatenate([high, low], axis=0), shift, preferred_element_type=F32
        )
        count = high.shape[0]
        return stacked[:count] + stacked[count:]

    def signed(octant):
        return signs_ref[octant : octant + 1, :]

    sign_rows = jnp.concatenate(
        [jnp.broadcast_to(signed(o)[:, 0:256], (64, 256)) for o in range(8)], axis=0
    )
    high = (sons[:, 0:256] * sign_rows).astype(BF16)
    low = (sons[:, 256:512] * sign_rows).astype(BF16)
    parts = moved(high, low)
    level = parts[0:64] * signed(0)
    tail_sum = sons[0:64, 512:640]
    for o in range(1, 8):
        level = level + parts[64 * o : 64 * o + 64] * signed(o)
        tail_sum = tail_sum + sons[64 * o : 64 * o + 64, 512:640]
    tail_lane = lax.broadcasted_iota(jnp.int32, (1, 128), 1) < 30

    def with_tail(body, tail):
        added = body[:, 256:384] + jnp.where(tail_lane, tail * tiny, 0.0)
        return jnp.concatenate([body[:, 0:256], added], axis=1)

    level_1 = with_tail(level, tail_sum + pltpu.roll(tail_sum, 96, 1))
    sign_rows = jnp.concatenate(
        [jnp.broadcast_to(signed(o), (8, 384)) for o in range(8)], axis=0
    )
    parts = moved(*split(level_1[:, 0:256] * sign_rows[:, 0:256])) * sign_rows
    level = jnp.sum(parts.reshape(8, 8, 384), axis=0)
    tail_sum = jnp.sum(level_1[:, 256:384].reshape(8, 8, 128), axis=0)
    level_2 = with_tail(level, tail_sum)
    all_signs = signs_ref[...]
    parts = moved(*split(level_2[:, 0:256] * all_signs[:, 0:256])) * all_signs
    level = jnp.sum(parts, axis=0, keepdims=True)
    tail_sum = jnp.sum(level_2[:, 256:384], axis=0, keepdims=True)
    level_3 = with_tail(level, tail_sum)
    sublane = lax.broadcasted_iota(jnp.int32, (8, 384), 0)

    def share(value, octant):
        sign = jnp.sum(jnp.where(sublane == octant, all_signs, 0.0), axis=0, keepdims=True)
        eight = jnp.broadcast_to(value * sign, (8, 384))
        part = moved(*split(eight[:, 0:256]))[0:1] * sign
        return with_tail(part, value[:, 256:384])

    level_4 = share(level_3, group % 8)
    level_5 = share(level_4, group // 8)
    send_ref[0:1] = level_4
    send_ref[1:2] = level_5
    level_ref[0:64] = level_1
    level_ref[64:72] = level_2
    level_ref[72:80] = jnp.broadcast_to(level_3, (8, 384))
    span_ref[0:1] = jnp.broadcast_to(start, (1, 128))
    span_ref[1:2] = jnp.broadcast_to(start + tally, (1, 128))
    span_ref[2:3] = jnp.zeros((1, 128), jnp.int32) + jnp.where(group % 8 == 0, 22, -1)
    span_ref[3:4] = jnp.zeros((1, 128), jnp.int32) + jnp.where(group == 0, 24, -1)


def outputs_kernel(got_ref, rank_ref, level_ref, span_ref, leaf_ref, box_ref):
    start = span_ref[0:1, 0:1]
    end = span_ref[1:2, 0:1]
    slot = start + lax.broadcasted_iota(jnp.int32, (128, 1), 0)
    chosen = jnp.where(jnp.where(slot < end, slot, -1) == rank_ref[...], 1.0, 0.0).astype(BF16)
    own = jnp.dot(chosen, group_values(got_ref), preferred_element_type=F32)
    own_tail = own[:, 512:640]
    leaf_ref[0:128] = (own[:, 0:128] + own[:, 256:384]).T
    leaf_ref[128:256] = (own[:, 128:256] + own[:, 384:512]).T
    leaf_ref[256:COEFS] = (own_tail + pltpu.roll(own_tail, 96, 1)).T[0 : COEFS - 256]
    out_slot = lax.broadcasted_iota(jnp.int32, (32, 1), 0)
    box_1 = start // 8 + out_slot
    box_2 = start // 64 + out_slot - 17
    source = jnp.where((box_1 * 8 >= start) & (box_1 * 8 < end), (box_1 % 8) * 8 + box_1 // 8, -1)
    source_2 = jnp.where((box_2 * 64 >= start) & (box_2 * 64 < end), 64 + box_2, -1)
    first_of_group = (start == 0) & (end > 0)
    source_3 = jnp.where(first_of_group & (out_slot == 20), 72, -1)
    source = jnp.where(out_slot < 17, source, jnp.where(out_slot < 20, source_2, source_3))
    column = lax.broadcasted_iota(jnp.int32, (32, 128), 1)
    select = jnp.where(column == source, 1.0, 0.0).astype(BF16)
    boxes = jnp.concatenate([level_ref[...], jnp.zeros((48, 384), F32)], axis=0)
    high, low = split(boxes)
    picked = jnp.dot(select, high, preferred_element_type=F32) + jnp.dot(
        select, low, preferred_element_type=F32
    )
    upper = (out_slot == span_ref[2:3, 0:1]) | (out_slot == span_ref[3:4, 0:1])
    owned = first_of_group & upper
    picked = picked + jnp.where(owned, 1.0, 0.0)
    box_ref[...] = picked[0:26, 0:COEFS]


def permute(value, *pairs):
    return lax.ppermute(value, "wide", list(pairs))


def across(share, got, kept):
    four = permute(share, *((8 + i, i) for i in range(6)))
    pair = share + permute(share, *((2 * i + 1, 2 * i) for i in range(16)))
    eight = permute(pair, (16, 0))
    nine = permute(pair, (18, 1), (20, 0))
    seven = permute(pair, (14, 0), (22, 1))
    twelve = permute(pair, (24, 0), (26, 1))
    after, four, kept = lax.optimization_barrier((pair, four, kept))
    fourteen = permute(after, (28, 0), (30, 1))
    quads = [[8 * q + j for j in range(8)] for q in range(4)]
    row = lax.broadcasted_iota(jnp.int32, (8, 2, 384), 1)
    spread = share[None] + jnp.where(row == 0, 0.0, four[None])
    quad = jnp.sum(
        lax.all_to_all(spread, "wide", 0, 0, axis_index_groups=quads, tiled=True), axis=0
    )
    leaf, box = outputs(got, *kept)
    late = seven + twelve + nine + fourteen
    return quad, quad + late + eight + permute(late, (1, 0)), leaf, box


VMEM = pl.BlockSpec(memory_space=pltpu.VMEM)
HBM = pl.BlockSpec(memory_space=pltpu.HBM)
SMEM = pl.BlockSpec(memory_space=pltpu.SMEM)
PARAMS = pltpu.CompilerParams(vmem_limit_bytes=40 * 1024 * 1024)


def outputs(got, rank, levels, span):
    return pl.pallas_call(
        outputs_kernel,
        out_shape=(
            jax.ShapeDtypeStruct((COEFS, 128), F32),
            jax.ShapeDtypeStruct((26, COEFS), F32),
        ),
        in_specs=[VMEM] * 4,
        out_specs=(VMEM,) * 2,
        compiler_params=PARAMS,
    )(got, rank, levels, span)


def shards(positions, moments, counts, dest):
    shift, signs = tables()
    where = jnp.stack([lax.axis_index("narrow"), lax.axis_index("wide")]).astype(jnp.int32)
    sent = pl.pallas_call(
        moments_kernel,
        out_shape=jax.ShapeDtypeStruct((16, 72, 128), F32),
        in_specs=[HBM] * 4,
        out_specs=HBM,
        scratch_shapes=[
            pltpu.VMEM((3, 32, 256), F32),
            pltpu.VMEM((3, 32, 256), F32),
            pltpu.VMEM((1, 32), jnp.int32),
            pltpu.VMEM((1, 32), jnp.int32),
            pltpu.VMEM((72, 128), F32),
            pltpu.VMEM((6, 64, 128), F32),
            pltpu.VMEM((288, 8, 128), F32),
            pltpu.SemaphoreType.DMA((8,)),
            pltpu.SemaphoreType.DMA((16,)),
        ],
        compiler_params=pltpu.CompilerParams(vmem_limit_bytes=64 * 1024 * 1024 - 65536),
    )(
        jnp.transpose(positions, (1, 0, 2)),
        jnp.transpose(moments, (1, 0, 2)),
        counts.reshape(1, 32),
        dest.reshape(1, 32),
    )
    got = lax.all_to_all(sent, "narrow", split_axis=0, concat_axis=0, tiled=True)
    share, *kept = pl.pallas_call(
        tree_kernel,
        out_shape=(
            jax.ShapeDtypeStruct((2, 384), F32),
            jax.ShapeDtypeStruct((1, GROUP), jnp.int32),
            jax.ShapeDtypeStruct((80, 384), F32),
            jax.ShapeDtypeStruct((4, 128), jnp.int32),
        ),
        in_specs=[SMEM, VMEM, VMEM, VMEM],
        out_specs=(VMEM,) * 4,
        compiler_params=PARAMS,
    )(where, got, jnp.asarray(shift, BF16), jnp.asarray(signs, F32))
    quad, top, leaf, box = across(share, got, kept)
    row = lax.broadcasted_iota(jnp.int32, (26, COEFS), 0)
    last = jnp.where(row == 24, top[1:2, 0:COEFS], 1.0)
    box = box * jnp.where(row == 22, quad[0:1, 0:COEFS], last)
    return leaf.T, box


def solution(mesh):
    both = ("wide", "narrow")
    placed = (P(both, None, None), P(both, None, None), P(both), P(both))
    return jax.shard_map(
        shards,
        mesh=mesh,
        in_specs=placed,
        out_specs=(P(both, None), P(both, None)),
        check_vma=False,
    )
```
